32 devices in a mesh: dp: 4 (over x, core), adapter: 8 (over z, y).
Axes of the slice: x: 2, y: 2, z: 4, core: 2. Of those that a mesh axis runs over, the one named last changes fastest.
Arguments:
- tokens: bfloat16 [4096, 8192], P(('dp', 'adapter')), may hold values from -6 to 6
- token_adapter_index: int32 [4096, 1], P(('dp', 'adapter')), may hold values from 0 to 31; in each aligned block of 128 rows (0 to 127, 128 to 255, ...) at most 8 rows name the same one
- frozen_value_weight: bfloat16 [8192, 1024], P('dp'), may hold values from -0.0625 to 0.0625
- adapter_down_factors: bfloat16 [128, 16, 8192], P(('dp', 'adapter')), may hold values from -0.0625 to 0.0625
- adapter_up_factors: bfloat16 [128, 16, 1024], P(('dp', 'adapter')), may hold values from -1.5 to 1.5
- output_gradient: bfloat16 [4096, 1024], P(('dp', 'adapter')), may hold values from -6 to 6
Outputs:
- result: bfloat16 [4096, 1024], P(('dp', 'adapter'))
- token_grad: bfloat16 [4096, 8192], P(('dp', 'adapter'))
- down_grad: float32 [128, 16, 8192], P(('dp', 'adapter'))
- up_factor_gradient: float32 [128, 16, 1024], P(('dp', 'adapter'))
The draws below stay inside these ranges and needn't reach their ends.
Inputs may be any that keep to these rules, and one draw needn't show every extreme that they name: `token_adapter_index`: among one device's 128 tokens no adapter id appears more than 8 times; in some device one appears exactly 8 times.
All inputs are finite; a program needn't handle non-finite values.
Results may differ from the reference program's by a relative error of at most 0.0054.
Values may be sent and summed in bfloat16 or wider, within the bound.
A program may use at most 128 MiB of HBM per device.

```python
import math
import jax
import jax.numpy as jnp
import numpy as np
from jax import lax

MODEL_WIDTH = 8192
VALUE_WIDTH = 1024
ADAPTER_RANK = 16
ADP_DEV = 4
TOK_DEV = 128
MOST = 8
ADAPTER_TOTAL = 128
TOKENS = 4096
N_ADAPTER = 8


def shard_levels(stream_key, dims, cuts, least, largest):
    def one(axis_at, shards_of):
        steps = jax.random.uniform(jax.random.fold_in(jax.random.fold_in(stream_key, 6), axis_at), (shards_of,), jnp.float32, least / len(cuts), largest / len(cuts))
        return jnp.repeat(jnp.exp(steps), dims[axis_at] // shards_of).reshape((-1,) + (1,) * (len(dims) - axis_at - 1))

    factor_of = one(*cuts[0])
    for cut in cuts[1:]:
        factor_of = factor_of * one(*cut)
    return factor_of


def shared_out(rng, own, number, rows, amount, top, bound, lean):
    order = jax.random.permutation(rng, amount)
    packed, usual = shares(amount, rows * top, bound, lean, True), shares(amount, rows * top, bound, lean, False)
    places = jnp.arange(amount)

    def named(tallies, offset_by):
        used = int((tallies > 0).sum())
        fixed = max(1, used // 4)
        moved = fixed + (places - fixed + offset_by * (used - fixed)) % max(1, amount - fixed)
        return jnp.zeros((amount,), jnp.int32).at[order[jnp.where(places < fixed, places, moved)]].set(jnp.asarray(tallies, jnp.int32))

    tallies = jnp.where(number % 4 == 0, named(packed, number // 4), named(usual, number - number // 4 - 1))
    mixed = jax.random.permutation(jax.random.fold_in(own, 3), amount)
    source_of, sink = mixed[0:amount // 2 * 2:2], mixed[1:amount // 2 * 2:2]
    margin = jnp.minimum(tallies[source_of] - 1, bound - tallies[sink]) // 2
    margin = jnp.where((source_of == order[0]) | (sink == order[0]) | (tallies[sink] == 0), 0, jnp.maximum(margin, 0))
    moved = jax.random.randint(jax.random.fold_in(own, 4), (amount // 2,), 0, 1 << 20) % (margin + 1)
    tallies = tallies.at[source_of].add(-moved).at[sink].add(moved)
    labels = jnp.searchsorted(jnp.cumsum(tallies), jnp.arange(rows * top), side="right").astype(jnp.int32)
    table = labels.reshape(top, rows).T
    table = table[jax.random.permutation(jax.random.fold_in(own, 1), rows)]
    offset_by = jax.random.randint(jax.random.fold_in(own, 2), (rows, 1), 0, top)
    return jnp.take_along_axis(table, (jnp.arange(top)[None, :] + offset_by) % top, axis=1)


def shares(count, total, reach, slope, full):
    loads = [(1 << 20) // math.isqrt(grade ** slope) + 1 for grade in range(1, count + 1)]
    largest = reach if full else min(reach, max(-(-total // count), total * loads[0] // sum(loads)))
    least = 1 if total - largest >= count - 1 else 0
    counts, surplus = [largest] + [least] * (count - 1), total - largest - least * (count - 1)
    while surplus > 0:
        candidates = [i for i in range(1, count) if counts[i] < largest] or [i for i in range(1, count) if counts[i] < reach]
        pool, budget = sum([loads[i] for i in candidates]), surplus
        for i in candidates:
            addition = min(reach - counts[i], max(1, budget * loads[i] // pool), surplus)
            counts[i] = counts[i] + addition
            surplus = surplus - addition
    return np.array(counts)


def scatter_about(stream_key, shape, scale, reach, shards=(), held_as=jnp.bfloat16):
    drawn = jax.random.normal(stream_key, shape, jnp.float32) * scale
    if len(shards) > 0:
        drawn = shard_levels(stream_key, shape, shards, -0.22, 0.18) * drawn
    return jnp.clip(drawn, min=-reach, max=reach).astype(held_as)


def setup_inputs(seed: int = 0) -> dict:
    arg_keys = jax.random.split(jax.random.key(seed), 7)
    tokens = scatter_about(arg_keys[0], (TOKENS, MODEL_WIDTH), 1.0, 6.0, ((0, 32),))
    token_adapter_index_keys = jax.random.split(jax.random.fold_in(arg_keys[1], 1), TOKENS // TOK_DEV)
    token_adapter_index_turns = jax.random.permutation(jax.random.fold_in(arg_keys[1], 3), TOKENS // TOK_DEV)
    token_adapter_index = jax.vmap(lambda own, number: shared_out(jax.random.fold_in(arg_keys[1], 2), own, number, TOK_DEV, ADP_DEV * N_ADAPTER, 1, MOST, 2))(token_adapter_index_keys, token_adapter_index_turns).reshape((TOKENS, 1))
    frozen_value_weight = scatter_about(arg_keys[2], (MODEL_WIDTH, VALUE_WIDTH), MODEL_WIDTH ** -0.5, 0.0625, ((0, 4),))
    adapter_down_factors = scatter_about(arg_keys[3], (ADAPTER_TOTAL, ADAPTER_RANK, MODEL_WIDTH), MODEL_WIDTH ** -0.5, 0.0625, ((0, 32),))
    adapter_up_factors = scatter_about(arg_keys[4], (ADAPTER_TOTAL, ADAPTER_RANK, VALUE_WIDTH), ADAPTER_RANK ** -0.5, 1.5, ((0, 32),))
    output_gradient = scatter_about(arg_keys[5], (TOKENS, VALUE_WIDTH), 1.0, 6.0, ((0, 32),))
    return dict(tokens=tokens, token_adapter_index=token_adapter_index, frozen_value_weight=frozen_value_weight, adapter_down_factors=adapter_down_factors, adapter_up_factors=adapter_up_factors, output_gradient=output_gradient)


adapter_scale = 2.0


def reference(tokens, token_adapter_index, frozen_value_weight, adapter_down_factors, adapter_up_factors, output_gradient):
    group_count = ADP_DEV * N_ADAPTER
    blocks = TOKENS // TOK_DEV
    base = jnp.dot(tokens, frozen_value_weight, preferred_element_type=jnp.float32)
    back = lax.dot_general(output_gradient, frozen_value_weight, (((1,), (1,)), ((), ())), preferred_element_type=jnp.float32)
    token_ids = token_adapter_index[:, 0].astype(jnp.int32).reshape(blocks, TOK_DEV)
    group_base = (jnp.arange(blocks, dtype=jnp.int32) // N_ADAPTER) * group_count
    global_ids = (token_ids + group_base[:, None]).astype(jnp.int32)

    def step(carry, inputs):
        down_acc, up_acc = carry
        rows, gradient_list, adapter_index = inputs
        down_factor = adapter_down_factors[adapter_index].astype(jnp.float32)
        up_factor = adapter_up_factors[adapter_index].astype(jnp.float32)
        rows32 = rows.astype(jnp.float32)
        gradient_list_fp32 = gradient_list.astype(jnp.float32)
        rank_rows = jnp.einsum('td,trd->tr', rows32, down_factor).astype(jnp.bfloat16).astype(jnp.float32)
        raised_rows = (adapter_scale * jnp.einsum('wu,wui->wi', rank_rows, up_factor)).astype(jnp.bfloat16)
        rank_gradient = (adapter_scale * jnp.einsum('ym,ydm->yd', gradient_list_fp32, up_factor)).astype(jnp.bfloat16).astype(jnp.float32)
        side = jnp.einsum('tr,trd->td', rank_gradient, down_factor).astype(jnp.bfloat16)
        down_acc = down_acc.at[adapter_index].add(jnp.einsum('tr,td->trd', rank_gradient, rows32))
        up_acc = up_acc.at[adapter_index].add(jnp.einsum('tr,tk->trk', rank_rows, gradient_list_fp32))
        return (down_acc, up_acc), (raised_rows, side)

    start = (jnp.zeros((ADAPTER_TOTAL, ADAPTER_RANK, MODEL_WIDTH), jnp.float32), jnp.zeros((ADAPTER_TOTAL, ADAPTER_RANK, VALUE_WIDTH), jnp.float32))
    (down_grad, up_gradient_sum), (raised_rows, side) = lax.scan(
        step, start,
        (tokens.reshape(blocks, TOK_DEV, MODEL_WIDTH), output_gradient.reshape(blocks, TOK_DEV, VALUE_WIDTH), global_ids))
    up_factor_gradient = adapter_scale * up_gradient_sum
    result = (base + raised_rows.reshape(TOKENS, VALUE_WIDTH).astype(jnp.float32)).astype(jnp.bfloat16)
    token_grad = (back + side.reshape(TOKENS, MODEL_WIDTH).astype(jnp.float32)).astype(jnp.bfloat16)
    return result, token_grad, down_grad, up_factor_gradient
```

```python
import functools

import jax
import jax.numpy as jnp
from jax import lax
from jax.experimental import pallas as pl
from jax.experimental.pallas import tpu as pltpu
from jax.sharding import PartitionSpec as P

adapter_scale = 2.0
NT = (((1,), (1,)), ((), ()))


def grid_sides(owners):
    ny = 1
    while (2 * ny) ** 2 <= owners:
        ny *= 2
    return owners // ny, ny


def exchange_kernel(
    nz, ny, rank, tile,
    idx_ref, a_ref, b_ref, x_ref, og_ref,
    a_all, b_all, x_all, og_all, lg_t, low_all, dg_own, dg_in, up_own, up_in,
    gbuf, rin, rin2, ubuf, uin, uin2, low_part, low_in, dg_out, up_out,
    loc_sem, ag_send, ag_recv, b_send, b_recv, y_send, y_recv,
    rs_send, rs_recv, rs_recv2, us_send, us_recv, us_recv2,
):
    me = lax.axis_index("adapter")
    z = me // ny
    y = lax.rem(me, ny)
    rows = a_ref.shape[1]
    width = a_ref.shape[2]
    vcols = ubuf.shape[2]
    owned = rows // rank

    def peer(d):
        return lax.rem(y + d, ny)

    def copy_to(src, dst, ssem, rsem, dev):
        return pltpu.make_async_remote_copy(
            src_ref=src, dst_ref=dst, send_sem=ssem, recv_sem=rsem,
            device_id={"adapter": dev}, device_id_type=pl.DeviceIdType.MESH,
        )

    barrier = pltpu.get_barrier_semaphore()

    def greet(dev):
        pl.semaphore_signal(
            barrier, inc=1, device_id={"adapter": dev}, device_id_type=pl.DeviceIdType.MESH
        )

    for d in range(1, ny):
        greet(z * ny + peer(d))
    pl.when(z > 0)(lambda: greet(me - ny))
    pl.when(z < nz - 1)(lambda: greet(me + ny))
    pl.semaphore_wait(
        barrier,
        (ny - 1) + jnp.where(z > 0, 1, 0) + jnp.where(z < nz - 1, 1, 0),
    )

    def y_copy(kind, d, src, dst):
        return copy_to(
            src, dst, y_send.at[kind, d - 1], y_recv.at[kind, d - 1], z * ny + peer(d)
        )

    def y_wait(kind, d, dst):
        copy_to(
            dst, dst, y_send.at[kind, d - 1], y_recv.at[kind, d - 1], z * ny + peer(ny - d)
        ).wait_recv()

    sends = []

    def y_start(kind, d, src, dst):
        c = y_copy(kind, d, src, dst)
        c.start()
        sends.append(c)

    for d in range(1, ny):
        y_start(0, d, b_ref, b_all.at[me])
    for d in range(1, ny):
        y_start(1, d, x_ref.at[peer(d)], x_all.at[y])
    for d in range(1, ny):
        y_start(2, d, a_ref.at[peer(d)], a_all.at[me])
    for d in range(1, ny):
        y_start(3, d, og_ref, og_all.at[y])
    local = [
        pltpu.make_async_copy(b_ref, b_all.at[me], loc_sem.at[0]),
        pltpu.make_async_copy(a_ref.at[y], a_all.at[me], loc_sem.at[1]),
        pltpu.make_async_copy(x_ref.at[y], x_all.at[y], loc_sem.at[2]),
        pltpu.make_async_copy(og_ref, og_all.at[y], loc_sem.at[3]),
    ]
    for c in local:
        c.start()
    for c in local:
        c.wait()

    def hop(buf, ssem, rsem, s, ys, last=False):
        n_left = (z - s) * ny + ys
        n_right = (z + s) * ny + ys

        def right(start):
            c = copy_to(buf.at[n_left], buf.at[n_left], ssem.at[0, n_left], rsem.at[n_left], me + ny)
            c.start() if start else c.wait_send()

        def left(start):
            c = copy_to(
                buf.at[n_right], buf.at[n_right], ssem.at[1, n_right], rsem.at[n_right], me - ny
            )
            c.start() if start else c.wait_send()

        if last:
            pl.when((z >= s) & (z < nz - 1))(lambda: right(False))
            pl.when((z + s < nz) & (z > 0))(lambda: left(False))
            return
        if s > 0:
            @pl.when(z >= s)
            def _():
                copy_to(
                    buf.at[n_left], buf.at[n_left], ssem.at[0, n_left], rsem.at[n_left], me - ny
                ).wait_recv()
        pl.when((z >= s) & (z < nz - 1))(lambda: right(True))
        if s > 0:
            @pl.when(z + s < nz)
            def _():
                copy_to(
                    buf.at[n_right], buf.at[n_right], ssem.at[1, n_right], rsem.at[n_right], me + ny
                ).wait_recv()
        pl.when((z + s < nz) & (z > 0))(lambda: left(True))

    for s in range(nz):
        hop(b_all, b_send, b_recv, s, y)
        if s == 0:
            hop(a_all, ag_send, ag_recv, s, y)
        for d in range(1, ny):
            if s == 0:
                y_wait(0, d, b_all.at[z * ny + peer(ny - d)])
            hop(b_all, b_send, b_recv, s, peer(ny - d))
        if s > 0:
            hop(a_all, ag_send, ag_recv, s, y)

    def masked(dense, n):
        adapter = n * owned + lax.broadcasted_iota(jnp.int32, dense.shape, 0) // rank
        return jnp.where(adapter == idx_ref[...], dense, 0.0).astype(jnp.bfloat16)

    def lg_block(n, carry):
        dense = adapter_scale * lax.dot_general(
            b_all[n], og_ref[...], NT, preferred_element_type=jnp.float32
        )
        lg_t[y, n] = masked(dense, n)
        return carry

    lax.fori_loop(0, nz * ny, lg_block, 0)
    for d in range(1, ny):
        y_start(4, d, lg_t.at[y], lg_t.at[y])
    for d in range(1, ny):
        y_wait(1, d, x_all.at[peer(ny - d)])
        y_wait(4, d, lg_t.at[peer(ny - d)])

    def grad(coef, acts, n, total, step, put, extra=()):
        @pl.loop(0, total // step)
        def _(i):
            cols = pl.ds(pl.multiple_of(i * step, step), step)
            acc = jnp.dot(coef[0, n], acts(0, cols), preferred_element_type=jnp.float32)
            for j in range(1, ny):
                acc += jnp.dot(coef[j, n], acts(j, cols), preferred_element_type=jnp.float32)
            for ref, at in extra:
                acc += ref[at, :, cols].astype(jnp.float32)
            put(cols, acc)

    def x_acts(j, cols):
        return x_all[j, :, cols]

    def v_acts(j, cols):
        return og_all[j, :, pl.ds(pl.multiple_of(y * vcols, vcols), vcols)]

    def reduce_step(t, coef, acts, out, inbox, inbox2, ssem, rsem, rsem2, total, step, last=False):
        for right in (True, False):
            pos = z if right else nz - 1 - z
            zo = (nz - 1 - (t - z)) if right else (t - (nz - 1 - z))
            ahead = me + ny if right else me - ny
            behind = me - ny if right else me + ny

            @pl.when((pos <= t) & (pos < nz - 1))
            def _():
                for yo in range(ny):
                    n = zo * ny + yo
                    if right:
                        c = copy_to(out.at[n], inbox.at[n], ssem.at[n], rsem.at[n], ahead)
                        c2 = None
                    else:
                        c = copy_to(out.at[n], inbox.at[n], ssem.at[n], rsem.at[n], ahead)
                        c2 = copy_to(out.at[n], inbox2.at[yo], ssem.at[n], rsem2.at[yo], ahead)
                    if last:
                        c.wait_send()
                        continue

                    def put(cols, acc):
                        out[n, :, cols] = acc.astype(jnp.bfloat16)

                    @pl.when(pos == 0)
                    def _():
                        grad(coef, acts, n, total, step, put)

                    @pl.when(pos > 0)
                    def _():
                        copy_to(inbox.at[n], inbox.at[n], ssem.at[n], rsem.at[n], behind).wait_recv()
                        grad(coef, acts, n, total, step, put, ((inbox, n),))

                    if right:
                        c.start()
                    else:
                        pl.when(zo == z - 1)(lambda: c2.start())
                        pl.when(zo < z - 1)(lambda: c.start())

    def reduce_end(coef, acts, own, out, kind, inbox, inbox2, rsem, rsem2, total, step):
        for d in range(ny):
            yo = lax.rem(y + d, ny)
            n = z * ny + yo

            @pl.when(z > 0)
            def _():
                copy_to(inbox.at[n], inbox.at[n], rsem.at[n], rsem.at[n], me - ny).wait_recv()

            @pl.when(z < nz - 1)
            def _():
                copy_to(
                    inbox2.at[yo], inbox2.at[yo], rsem2.at[yo], rsem2.at[yo], me + ny
                ).wait_recv()

            def put(cols, acc):
                if d == 0:
                    own[:, cols] = acc
                else:
                    out[d - 1, :, cols] = acc.astype(jnp.bfloat16)

            first, second = (inbox, n), (inbox2, yo)

            @pl.when((z > 0) & (z < nz - 1))
            def _():
                grad(coef, acts, n, total, step, put, (first, second))

            @pl.when(z == 0)
            def _():
                grad(coef, acts, n, total, step, put, (second,))

            @pl.when(z == nz - 1)
            def _():
                grad(coef, acts, n, total, step, put, (first,))

    def low_block(n):
        for j in range(ny):
            low_part[j, n] = lax.dot_general(
                a_all[n], x_all[j], NT, preferred_element_type=jnp.float32
            )

    down = (lg_t, x_acts, gbuf, rin, rin2, rs_send, rs_recv, rs_recv2, width, tile)
    for s in range(nz):
        for d in range(1, ny):
            if s == 0:
                y_wait(2, d, a_all.at[z * ny + peer(ny - d)])
            hop(a_all, ag_send, ag_recv, s, peer(ny - d))
        if s < nz - 1:
            reduce_step(s, *down)
        for yb in range(ny):
            pl.when(z >= s)(lambda: low_block((z - s) * ny + yb))
            if s > 0:
                pl.when(z + s < nz)(lambda: low_block((z + s) * ny + yb))

    for d in range(1, ny):
        y_start(5, d, low_part.at[peer(d)], low_in.at[d - 1])
    for d in range(1, ny):
        y_wait(5, d, low_in.at[d - 1])

    def low_sum(n, carry):
        total = low_part[y, n]
        for d in range(1, ny):
            total += low_in[d - 1, n]
        low_all[y, n] = masked(total, n)
        return carry

    lax.fori_loop(0, nz * ny, low_sum, 0)
    for d in range(1, ny):
        y_start(6, d, low_all.at[y], low_all.at[y])
    for d in range(1, ny):
        y_wait(3, d, og_all.at[peer(ny - d)])
        y_wait(6, d, low_all.at[peer(ny - d)])

    up = (low_all, v_acts, ubuf, uin, uin2, us_send, us_recv, us_recv2, vcols, vcols)
    for t in range(nz - 1):
        reduce_step(t, *up)
    reduce_end(lg_t, x_acts, dg_own, dg_out, 7, rin, rin2, rs_recv, rs_recv2, width, tile)
    for d in range(1, ny):
        y_start(7, d, dg_out.at[d - 1], dg_in.at[y])
    reduce_end(low_all, v_acts, up_own, up_out, 8, uin, uin2, us_recv, us_recv2, vcols, vcols)
    for d in range(1, ny):
        y_start(8, d, up_out.at[d - 1], up_in.at[y])
    dg_in[y] = jnp.zeros((rows, width), jnp.bfloat16)
    up_in[y] = jnp.zeros((rows, vcols), jnp.bfloat16)
    for d in range(1, ny):
        y_wait(7, d, dg_in.at[peer(ny - d)])
        y_wait(8, d, up_in.at[peer(ny - d)])

    for c in sends:
        c.wait_send()
    for s in range(nz):
        for d in range(ny):
            hop(b_all, b_send, b_recv, s, peer(d), last=True)
            hop(a_all, ag_send, ag_recv, s, peer(d), last=True)
    for t in range(nz - 1):
        reduce_step(t, *down, last=True)
        reduce_step(t, *up, last=True)


def exchange(nz, ny, rank, idx, a_cols, b_rows, x_cols, grads):
    nb = nz * ny
    _, rows, width = a_cols.shape
    tok_rows = x_cols.shape[1]
    kv_width = grads.shape[1]
    vcols = kv_width // ny
    bf, f32 = jnp.bfloat16, jnp.float32
    peers = max(1, ny - 1)
    outs = [
        ((nb, rows, width), bf),
        ((nb, rows, kv_width), bf),
        ((ny, tok_rows, width), bf),
        ((ny, tok_rows, kv_width), bf),
        ((ny, nb, rows, tok_rows), bf),
        ((ny, nb, rows, tok_rows), bf),
        ((rows, width), f32),
        ((ny, rows, width), bf),
        ((rows, vcols), f32),
        ((ny, rows, vcols), bf),
    ]
    vmem = pl.BlockSpec(memory_space=pltpu.VMEM)
    dma = pltpu.SemaphoreType.DMA
    return pl.pallas_call(
        functools.partial(exchange_kernel, nz, ny, rank, min(512, width)),
        out_shape=[jax.ShapeDtypeStruct(s, t) for s, t in outs],
        in_specs=[vmem] * 5,
        out_specs=[vmem] * len(outs),
        scratch_shapes=[
            pltpu.VMEM((nb, rows, width), bf),
            pltpu.VMEM((nb, rows, width), bf),
            pltpu.VMEM((ny, rows, width), bf),
            pltpu.VMEM((nb, rows, vcols), bf),
            pltpu.VMEM((nb, rows, vcols), bf),
            pltpu.VMEM((ny, rows, vcols), bf),
            pltpu.VMEM((ny, nb, rows, tok_rows), f32),
            pltpu.VMEM((peers, nb, rows, tok_rows), f32),
            pltpu.VMEM((peers, rows, width), bf),
            pltpu.VMEM((peers, rows, vcols), bf),
            dma((4,)),
            dma((2, nb)),
            dma((nb,)),
            dma((2, nb)),
            dma((nb,)),
            dma((9, peers)),
            dma((9, peers)),
            dma((nb,)),
            dma((nb,)),
            dma((ny,)),
            dma((nb,)),
            dma((nb,)),
            dma((ny,)),
        ],
        compiler_params=pltpu.CompilerParams(
            collective_id=0, has_side_effects=True, vmem_limit_bytes=60 * 1024 * 1024
        ),
    )(idx, a_cols, b_rows, x_cols, grads)


def local(
    tokens,
    token_adapter_index,
    frozen_value_weight,
    adapter_down_factors,
    adapter_up_factors,
    output_gradient,
):
    owners = lax.axis_size("adapter")
    shards = lax.axis_size("dp")
    nz, ny = grid_sides(owners)
    owned, rank, width = adapter_down_factors.shape
    tok_rows = tokens.shape[0]
    kv_width = output_gradient.shape[1]
    part = frozen_value_weight.shape[0] // ny
    y = lax.rem(lax.axis_index("adapter"), ny)

    def grouped(rows):
        return (
            rows.reshape(-1, shards, ny, part).transpose(2, 0, 1, 3).reshape(ny, -1, shards * part)
        )

    def joined(groups):
        return groups.reshape(ny, -1, shards, part).transpose(1, 2, 0, 3).reshape(-1, width)

    own_weight = lax.dynamic_slice_in_dim(frozen_value_weight, y * part, part, 0)
    weight = lax.all_gather(own_weight, "dp", axis=0, tiled=True)

    a_all, b_all, x_all, og_all, lg_t, low_all, dg_own, dg_in, up_own, up_in = exchange(
        nz, ny, rank,
        token_adapter_index.reshape(1, tok_rows),
        grouped(adapter_down_factors.reshape(owned * rank, width)),
        adapter_up_factors.reshape(owned * rank, kv_width),
        grouped(tokens),
        output_gradient,
    )
    slots = owners * owned * rank
    a_flat = a_all.reshape(slots, shards * part)
    pairs = {
        d: [(z * ny + i, z * ny + (i + d) % ny) for z in range(nz) for i in range(ny)]
        for d in range(1, ny)
    }

    def grads_of(j):
        lg = lax.dynamic_index_in_dim(lg_t, j, 0, False).reshape(slots, tok_rows)
        og = lax.dynamic_index_in_dim(og_all, j, 0, False)
        side = lax.dot_general(
            lg, a_flat, (((0,), (0,)), ((), ())), preferred_element_type=jnp.float32
        ).astype(jnp.bfloat16)
        back = lax.dot_general(
            og, weight, (((1,), (1,)), ((), ())), preferred_element_type=jnp.float32
        )
        return (back + side).astype(jnp.bfloat16)

    def base_of(j):
        x = lax.dynamic_index_in_dim(x_all, j, 0, False)
        return jnp.dot(x, weight, preferred_element_type=jnp.float32)

    grad_parts = jnp.zeros((ny, tok_rows, shards * part), jnp.bfloat16)
    base = base_of(y)
    for d in range(1, ny):
        to = lax.rem(y + d, ny)
        got = lax.ppermute(grads_of(to), "adapter", pairs[d])
        grad_parts = lax.dynamic_update_index_in_dim(grad_parts, got, lax.rem(y + ny - d, ny), 0)
        base += lax.ppermute(base_of(to).astype(jnp.bfloat16), "adapter", pairs[d]).astype(
            jnp.float32
        )
    grad_parts = lax.dynamic_update_index_in_dim(grad_parts, grads_of(y), y, 0)
    token_grad = joined(grad_parts)
    low_own = lax.dynamic_index_in_dim(low_all, y, 0, False).reshape(slots, tok_rows)
    lifted = (
        adapter_scale
        * lax.dot_general(
            low_own, b_all.reshape(slots, kv_width), (((0,), (0,)), ((), ())),
            preferred_element_type=jnp.float32,
        )
    ).astype(jnp.bfloat16)
    result = (base + lifted).astype(jnp.bfloat16)

    own = jnp.arange(ny)[:, None, None] == y
    down_grad = joined(jnp.where(own, dg_own[None], dg_in.astype(jnp.float32)))
    up_groups = adapter_scale * jnp.where(own, up_own[None], up_in.astype(jnp.float32))
    up_factor_gradient = up_groups.transpose(1, 0, 2).reshape(owned, rank, kv_width)
    return (result, token_grad, down_grad.reshape(owned, rank, width), up_factor_gradient)


def solution(mesh):
    in_specs = (
        P(("dp", "adapter"), None),
        P(("dp", "adapter"), None),
        P("dp", None),
        P(("dp", "adapter"), None, None),
        P(("dp", "adapter"), None, None),
        P(("dp", "adapter"), None),
    )
    out_specs = (
        P(("dp", "adapter"), None),
        P(("dp", "adapter"), None),
        P(("dp", "adapter"), None, None),
        P(("dp", "adapter"), None, None),
    )
    return jax.shard_map(local, mesh=mesh, in_specs=in_specs, out_specs=out_specs, check_vma=False)
```

```python
import functools

import jax
import jax.numpy as jnp
from jax import lax
from jax.experimental import pallas as pl
from jax.experimental.pallas import tpu as pltpu
from jax.sharding import PartitionSpec as P

adapter_scale = 2.0
NT = (((1,), (1,)), ((), ()))


def grid_sides(owners):
    ny = 1
    while (2 * ny) ** 2 <= owners:
        ny *= 2
    return owners // ny, ny


def exchange_kernel(
    nz, ny, rank, shards, tile,
    idx_ref, a_ref, b_ref, x_ref, og_ref,
    a_all, b_all, x_all, og_all, lg_t, low_all, dg_full, up_full,
    gbuf, rin, rin2, ubuf, uin, uin2, low_part, low_in, dg_out, dg_in, up_out, up_in,
    loc_sem, ag_send, ag_recv, b_send, b_recv, y_send, y_recv,
    rs_send, rs_recv, rs_recv2, us_send, us_recv, us_recv2,
):
    me = lax.axis_index("adapter")
    z = me // ny
    y = lax.rem(me, ny)
    rows, width = a_all.shape[1:]
    tok = og_ref.shape[0]
    part = width // shards
    vcols = ubuf.shape[2]
    owned = rows // rank
    nb = nz * ny

    def peer(d):
        return lax.rem(y + d, ny)

    def back(d):
        return lax.rem(y + ny - d, ny)

    def slot(j):
        return pl.ds(pl.multiple_of(j * tok, tok), tok)

    def copy_to(src, dst, ssem, rsem, dev):
        return pltpu.make_async_remote_copy(
            src_ref=src, dst_ref=dst, send_sem=ssem, recv_sem=rsem,
            device_id={"adapter": dev}, device_id_type=pl.DeviceIdType.MESH,
        )

    barrier = pltpu.get_barrier_semaphore()

    def greet(dev):
        pl.semaphore_signal(
            barrier, inc=1, device_id={"adapter": dev}, device_id_type=pl.DeviceIdType.MESH
        )

    for d in range(1, ny):
        greet(z * ny + peer(d))
    pl.when(z > 0)(lambda: greet(me - ny))
    pl.when(z < nz - 1)(lambda: greet(me + ny))
    pl.semaphore_wait(
        barrier,
        (ny - 1) + jnp.where(z > 0, 1, 0) + jnp.where(z < nz - 1, 1, 0),
    )

    sends = []

    def y_start(kind, d, src, dst):
        c = copy_to(
            src, dst, y_send.at[kind, d - 1], y_recv.at[kind, d - 1], z * ny + peer(d)
        )
        c.start()
        sends.append(c)

    def pieces(src, j, dst):
        for q in range(shards):
            at = pl.ds(pl.multiple_of((q * ny + j) * part, part), part)
            yield src.at[:, at], dst.at[:, pl.ds(q * part, part)]

    def y_start_columns(kind, d, src, dst):
        ssem, rsem, dev = y_send.at[kind, d - 1], y_recv.at[kind, d - 1], z * ny + peer(d)
        for piece, to in pieces(src, peer(d), dst):
            copy_to(piece, to, ssem, rsem, dev).start()
        sends.append(copy_to(dst, dst, ssem, rsem, dev))

    def y_wait(kind, d, dst):
        copy_to(
            dst, dst, y_send.at[kind, d - 1], y_recv.at[kind, d - 1], z * ny + back(d)
        ).wait_recv()

    for d in range(1, ny):
        y_start(0, d, b_ref, b_all.at[me])
    for d in range(1, ny):
        y_start_columns(1, d, x_ref, x_all.at[slot(y)])
    keep_b = pltpu.make_async_copy(b_ref, b_all.at[me], loc_sem.at[0])
    keep_og = pltpu.make_async_copy(og_ref, og_all.at[slot(y)], loc_sem.at[3])
    keep_b.start()
    for src, dst in pieces(a_ref, y, a_all.at[me]):
        pltpu.make_async_copy(src, dst, loc_sem.at[1]).start()
    for src, dst in pieces(x_ref, y, x_all.at[slot(y)]):
        pltpu.make_async_copy(src, dst, loc_sem.at[2]).start()
    keep_og.start()

    def hop(buf, ssem, rsem, s, ys, last=False):
        n_left = (z - s) * ny + ys
        n_right = (z + s) * ny + ys

        def right(start):
            c = copy_to(buf.at[n_left], buf.at[n_left], ssem.at[0, n_left], rsem.at[n_left], me + ny)
            c.start() if start else c.wait_send()

        def left(start):
            c = copy_to(
                buf.at[n_right], buf.at[n_right], ssem.at[1, n_right], rsem.at[n_right], me - ny
            )
            c.start() if start else c.wait_send()

        if last:
            pl.when((z >= s) & (z < nz - 1))(lambda: right(False))
            pl.when((z + s < nz) & (z > 0))(lambda: left(False))
            return
        if s > 0:
            @pl.when(z >= s)
            def _():
                copy_to(
                    buf.at[n_left], buf.at[n_left], ssem.at[0, n_left], rsem.at[n_left], me - ny
                ).wait_recv()
        pl.when((z >= s) & (z < nz - 1))(lambda: right(True))
        if s > 0:
            @pl.when(z + s < nz)
            def _():
                copy_to(
                    buf.at[n_right], buf.at[n_right], ssem.at[1, n_right], rsem.at[n_right], me + ny
                ).wait_recv()
        pl.when((z + s < nz) & (z > 0))(lambda: left(True))

    def hop_b(s):
        hop(b_all, b_send, b_recv, s, y)
        for d in range(1, ny):
            if s == 0:
                y_wait(0, d, b_all.at[z * ny + back(d)])
            hop(b_all, b_send, b_recv, s, back(d))

    def hop_own(s):
        hop(a_all, ag_send, ag_recv, s, y)

    def hop_peers(s):
        for d in range(1, ny):
            if s == 0:
                y_wait(2, d, a_all.at[z * ny + back(d)])
            hop(a_all, ag_send, ag_recv, s, back(d))

    keep_b.wait()
    hop_b(0)
    pltpu.make_async_copy(a_all.at[me], a_all.at[me], loc_sem.at[1]).wait()
    hop_own(0)
    hop_b(1)
    for s in range(2, nz):
        hop_b(s)
        if s < nz - 1:
            hop_own(s - 1)

    def masked(dense, n):
        adapter = n * owned + lax.broadcasted_iota(jnp.int32, dense.shape, 0) // rank
        return jnp.where(adapter == idx_ref[...], dense, 0.0).astype(jnp.bfloat16)

    def lg_block(n, carry):
        dense = adapter_scale * lax.dot_general(
            b_all[n], og_ref[...], NT, preferred_element_type=jnp.float32
        )
        lg_t[n, :, slot(y)] = masked(dense, n)
        return carry

    lax.fori_loop(0, nb, lg_block, 0)
    for d in range(1, ny):
        y_start(4, d, lg_t.at[:, :, slot(y)], lg_t.at[:, :, slot(y)])
    for d in range(1, ny):
        y_start_columns(2, d, a_ref, a_all.at[me])
    keep_og.wait()
    for d in range(1, ny):
        y_start(3, d, og_ref, og_all.at[slot(y)])
    pltpu.make_async_copy(x_all.at[slot(y)], x_all.at[slot(y)], loc_sem.at[2]).wait()
    for d in range(1, ny):
        y_wait(1, d, x_all.at[slot(back(d))])
        y_wait(4, d, lg_t.at[:, :, slot(back(d))])

    def grad(coef, acts, n, count, total, step, put, extra=()):
        blocks = pl.ds(n, count)

        @pl.loop(0, total // step)
        def _(i):
            start = pl.multiple_of(i * step, step)
            cols = pl.ds(start, step)
            acc = jnp.dot(
                coef[blocks].reshape(count * rows, coef.shape[2]), acts(cols),
                preferred_element_type=jnp.float32,
            )
            for ref, at in extra:
                acc += ref[pl.ds(at, count), :, cols].reshape(count * rows, step).astype(
                    jnp.float32
                )
            put(start, cols, acc)

    def x_acts(cols):
        return x_all[:, cols]

    def v_acts(cols):
        return og_all[:, pl.ds(pl.multiple_of(y * vcols, vcols), vcols)]

    def reduce_step(t, coef, acts, out, inbox, inbox2, ssem, rsem, rsem2, total, step, last=False):
        for right in (True, False):
            pos = z if right else nz - 1 - z
            zo = (nz - 1 - (t - z)) if right else (t - (nz - 1 - z))
            ahead = me + ny if right else me - ny
            behind = me - ny if right else me + ny

            @pl.when((pos <= t) & (pos < nz - 1))
            def _():
                blocks = pl.ds(zo * ny, ny)

                def send(dst, recv):
                    return copy_to(out.at[blocks], dst, ssem.at[zo], recv, ahead)

                if last:
                    send(inbox.at[blocks], rsem.at[zo]).wait_send()
                    return

                def put(start, cols, acc):
                    out[blocks, :, cols] = acc.astype(jnp.bfloat16).reshape(ny, rows, step)

                @pl.when(pos == 0)
                def _():
                    grad(coef, acts, zo * ny, ny, total, step, put)

                @pl.when(pos > 0)
                def _():
                    copy_to(
                        inbox.at[blocks], inbox.at[blocks], ssem.at[zo], rsem.at[zo], behind
                    ).wait_recv()
                    grad(coef, acts, zo * ny, ny, total, step, put, ((inbox, zo * ny),))

                if right:
                    send(inbox.at[blocks], rsem.at[zo]).start()
                else:
                    pl.when(zo == z - 1)(lambda: send(inbox2, rsem2.at[0]).start())
                    pl.when(zo < z - 1)(lambda: send(inbox.at[blocks], rsem.at[zo]).start())

    def reduce_end(coef, acts, own, out, inbox, inbox2, rsem, rsem2, total, step):
        blocks = pl.ds(z * ny, ny)

        @pl.when(z > 0)
        def _():
            copy_to(inbox.at[blocks], inbox.at[blocks], rsem.at[z], rsem.at[z], me - ny).wait_recv()

        @pl.when(z < nz - 1)
        def _():
            copy_to(inbox2, inbox2, rsem2.at[0], rsem2.at[0], me + ny).wait_recv()

        for d in range(1, ny + 1):
            yo = lax.rem(y + d, ny)
            n = z * ny + yo

            def put(start, cols, acc):
                if d == ny:
                    own(y, start, acc)
                else:
                    out[d - 1, :, cols] = acc.astype(jnp.bfloat16)

            first, second = (inbox, n), (inbox2, yo)

            @pl.when((z > 0) & (z < nz - 1))
            def _():
                grad(coef, acts, n, 1, total, step, put, (first, second))

            @pl.when(z == 0)
            def _():
                grad(coef, acts, n, 1, total, step, put, (second,))

            @pl.when(z == nz - 1)
            def _():
                grad(coef, acts, n, 1, total, step, put, (first,))

            yield d

    def down_at(j, start, values):
        q = start // part
        at = pl.multiple_of((q * ny + j) * part + start - q * part, tile)
        dg_full[:, pl.ds(at, tile)] = values

    def up_at(j, start, values):
        up_full[:, pl.ds(pl.multiple_of(j * vcols, vcols), vcols)] = adapter_scale * values

    down = (lg_t, x_acts, gbuf, rin, rin2, rs_send, rs_recv, rs_recv2, width, tile)
    up = (low_all, v_acts, ubuf, uin, uin2, us_send, us_recv, us_recv2, vcols, vcols)
    reduce_step(0, *down)
    if nz > 2:
        hop_own(nz - 2)
    hop_peers(0)
    for s in range(1, nz - 1):
        hop_peers(s)
        reduce_step(s, *down)
    hop_own(nz - 1)
    hop_peers(nz - 1)

    for j in range(ny):
        low_part[j] = jnp.zeros((nb * rows, tok), jnp.float32)

        @pl.loop(0, width // tile)
        def _(i):
            cols = pl.ds(pl.multiple_of(i * tile, tile), tile)
            low_part[j] += lax.dot_general(
                a_all[:, :, cols].reshape(nb * rows, tile), x_all[slot(j), cols], NT,
                preferred_element_type=jnp.float32,
            )

    for d in range(1, ny):
        y_start(5, d, low_part.at[peer(d)], low_in.at[d - 1])
    for d in range(1, ny):
        y_wait(5, d, low_in.at[d - 1])

    def low_sum(n, carry):
        at = pl.ds(pl.multiple_of(n * rows, rows), rows)
        total = low_part[y, at]
        for d in range(1, ny):
            total += low_in[d - 1, at]
        low_all[n, :, slot(y)] = masked(total, n)
        return carry

    lax.fori_loop(0, nb, low_sum, 0)
    for d in range(1, ny):
        y_start(6, d, low_all.at[:, :, slot(y)], low_all.at[:, :, slot(y)])
    for d in range(1, ny):
        y_wait(3, d, og_all.at[slot(back(d))])
        y_wait(6, d, low_all.at[:, :, slot(back(d))])

    for t in range(nz - 1):
        reduce_step(t, *up)
    for d in reduce_end(
        lg_t, x_acts, down_at, dg_out, rin, rin2, rs_recv, rs_recv2, width, tile
    ):
        if d < ny:
            y_start(7, d, dg_out.at[d - 1], dg_in.at[d - 1])
    for d in reduce_end(
        low_all, v_acts, up_at, up_out, uin, uin2, us_recv, us_recv2, vcols, vcols
    ):
        if d < ny:
            y_start(8, d, up_out.at[d - 1], up_in.at[d - 1])
    for d in range(1, ny):
        y_wait(8, d, up_in.at[d - 1])
        up_at(back(d), 0, up_in[d - 1].astype(jnp.float32))
    for d in range(1, ny):
        y_wait(7, d, dg_in.at[d - 1])

        @pl.loop(0, width // tile)
        def _(i):
            start = pl.multiple_of(i * tile, tile)
            down_at(back(d), start, dg_in[d - 1, :, pl.ds(start, tile)].astype(jnp.float32))

    for c in sends:
        c.wait_send()
    for s in range(nz):
        for d in range(ny):
            hop(b_all, b_send, b_recv, s, peer(d), last=True)
            hop(a_all, ag_send, ag_recv, s, peer(d), last=True)
    for t in range(nz - 1):
        reduce_step(t, *down, last=True)
        reduce_step(t, *up, last=True)


def exchange(nz, ny, shards, rank, idx, a_rows, b_rows, tokens, grads):
    nb = nz * ny
    rows = a_rows.shape[0]
    width = a_rows.shape[1] // ny
    tok_rows = tokens.shape[0]
    kv_width = grads.shape[1]
    vcols = kv_width // ny
    bf, f32 = jnp.bfloat16, jnp.float32
    peers = max(1, ny - 1)
    outs = [
        ((nb, rows, width), bf),
        ((nb, rows, kv_width), bf),
        ((ny * tok_rows, width), bf),
        ((ny * tok_rows, kv_width), bf),
        ((nb, rows, ny * tok_rows), bf),
        ((nb, rows, ny * tok_rows), bf),
        ((rows, ny * width), f32),
        ((rows, kv_width), f32),
    ]
    vmem = pl.BlockSpec(memory_space=pltpu.VMEM)
    dma = pltpu.SemaphoreType.DMA
    return pl.pallas_call(
        functools.partial(
            exchange_kernel, nz, ny, rank, shards, min(512, width // shards)
        ),
        out_shape=[jax.ShapeDtypeStruct(s, t) for s, t in outs],
        in_specs=[vmem] * 5,
        out_specs=[vmem] * len(outs),
        scratch_shapes=[
            pltpu.VMEM((nb, rows, width), bf),
            pltpu.VMEM((nb, rows, width), bf),
            pltpu.VMEM((ny, rows, width), bf),
            pltpu.VMEM((nb, rows, vcols), bf),
            pltpu.VMEM((nb, rows, vcols), bf),
            pltpu.VMEM((ny, rows, vcols), bf),
            pltpu.VMEM((ny, nb * rows, tok_rows), f32),
            pltpu.VMEM((peers, nb * rows, tok_rows), f32),
            pltpu.VMEM((peers, rows, width), bf),
            pltpu.VMEM((peers, rows, width), bf),
            pltpu.VMEM((peers, rows, vcols), bf),
            pltpu.VMEM((peers, rows, vcols), bf),
            dma((4,)),
            dma((2, nb)),
            dma((nb,)),
            dma((2, nb)),
            dma((nb,)),
            dma((9, peers)),
            dma((9, peers)),
            dma((nz,)),
            dma((nz,)),
            dma((1,)),
            dma((nz,)),
            dma((nz,)),
            dma((1,)),
        ],
        compiler_params=pltpu.CompilerParams(
            collective_id=0, has_side_effects=True, vmem_limit_bytes=60 * 1024 * 1024
        ),
    )(idx, a_rows, b_rows, tokens, grads)


def local(
    tokens,
    token_adapter_index,
    frozen_value_weight,
    adapter_down_factors,
    adapter_up_factors,
    output_gradient,
):
    owners = lax.axis_size("adapter")
    shards = lax.axis_size("dp")
    nz, ny = grid_sides(owners)
    owned, rank, width = adapter_down_factors.shape
    tok_rows = tokens.shape[0]
    kv_width = output_gradient.shape[1]
    part = frozen_value_weight.shape[0] // ny
    y = lax.rem(lax.axis_index("adapter"), ny)

    def joined(groups):
        return groups.reshape(ny, -1, shards, part).transpose(1, 2, 0, 3).reshape(-1, width)

    own_weight = lax.dynamic_slice_in_dim(frozen_value_weight, y * part, part, 0)
    weight = lax.all_gather(own_weight, "dp", axis=0, tiled=True)

    a_all, b_all, x_all, og_all, lg_t, low_all, down_grad, up_factor_gradient = exchange(
        nz, ny, shards, rank,
        token_adapter_index.reshape(1, tok_rows),
        adapter_down_factors.reshape(owned * rank, width),
        adapter_up_factors.reshape(owned * rank, kv_width),
        tokens,
        output_gradient,
    )
    slots = owners * owned * rank
    a_flat = a_all.reshape(slots, shards * part)
    pairs = {
        d: [(z * ny + i, z * ny + (i + d) % ny) for z in range(nz) for i in range(ny)]
        for d in range(1, ny)
    }

    def grads_of(j):
        lg = lax.dynamic_slice_in_dim(
            lg_t.reshape(slots, ny * tok_rows), j * tok_rows, tok_rows, 1
        )
        og = lax.dynamic_slice_in_dim(og_all, j * tok_rows, tok_rows, 0)
        side = lax.dot_general(
            lg, a_flat, (((0,), (0,)), ((), ())), preferred_element_type=jnp.float32
        ).astype(jnp.bfloat16)
        back = lax.dot_general(
            og, weight, (((1,), (1,)), ((), ())), preferred_element_type=jnp.float32
        )
        return (back + side).astype(jnp.bfloat16)

    def base_of(j):
        x = lax.dynamic_slice_in_dim(x_all, j * tok_rows, tok_rows, 0)
        return jnp.dot(x, weight, preferred_element_type=jnp.float32)

    grad_parts = jnp.zeros((ny, tok_rows, shards * part), jnp.bfloat16)
    base = base_of(y)
    for d in range(1, ny):
        to = lax.rem(y + d, ny)
        got = lax.ppermute(grads_of(to), "adapter", pairs[d])
        grad_parts = lax.dynamic_update_index_in_dim(grad_parts, got, lax.rem(y + ny - d, ny), 0)
        base += lax.ppermute(base_of(to).astype(jnp.bfloat16), "adapter", pairs[d]).astype(
            jnp.float32
        )
    grad_parts = lax.dynamic_update_index_in_dim(grad_parts, grads_of(y), y, 0)
    token_grad = joined(grad_parts)
    low_own = lax.dynamic_slice_in_dim(
        low_all.reshape(slots, ny * tok_rows), y * tok_rows, tok_rows, 1
    )
    lifted = (
        adapter_scale
        * lax.dot_general(
            low_own, b_all.reshape(slots, kv_width), (((0,), (0,)), ((), ())),
            preferred_element_type=jnp.float32,
        )
    ).astype(jnp.bfloat16)
    result = (base + lifted).astype(jnp.bfloat16)

    return (
        result,
        token_grad,
        down_grad.reshape(owned, rank, width),
        up_factor_gradient.reshape(owned, rank, kv_width),
    )


def solution(mesh):
    in_specs = (
        P(("dp", "adapter"), None),
        P(("dp", "adapter"), None),
        P("dp", None),
        P(("dp", "adapter"), None, None),
        P(("dp", "adapter"), None, None),
        P(("dp", "adapter"), None),
    )
    out_specs = (
        P(("dp", "adapter"), None),
        P(("dp", "adapter"), None),
        P(("dp", "adapter"), None, None),
        P(("dp", "adapter"), None, None),
    )
    return jax.shard_map(local, mesh=mesh, in_specs=in_specs, out_specs=out_specs, check_vma=False)
```

```python
import functools

import jax
import jax.numpy as jnp
from jax import lax
from jax.experimental import pallas as pl
from jax.experimental.pallas import tpu as pltpu
from jax.sharding import PartitionSpec as P

adapter_scale = 2.0
NT = (((1,), (1,)), ((), ()))


def grid_sides(owners):
    ny = 1
    while (2 * ny) ** 2 <= owners:
        ny *= 2
    return owners // ny, ny


def exchange_kernel(
    nz, ny, rank, tile,
    idx_ref, a_ref, b_ref, x_ref, og_ref,
    b_all, low_all, side_full, dg_full, up_full,
    a_all, x_all, og_all, lg_t, side_out, gbuf, rin, rin2, ubuf, uin, uin2, low_part, low_in, dg_out, dg_in, up_out, up_in,
    loc_sem, ag_send, ag_recv, b_send, b_recv, y_send, y_recv,
    rs_send, rs_recv, rs_recv2, us_send, us_recv, us_recv2,
):
    me = lax.axis_index("adapter")
    z = me // ny
    y = lax.rem(me, ny)
    rows, width = a_all.shape[1:]
    tok = og_ref.shape[0]
    vcols = ubuf.shape[2]
    owned = rows // rank
    nb = nz * ny

    def peer(d):
        return lax.rem(y + d, ny)

    def back(d):
        return lax.rem(y + ny - d, ny)

    def slot(j):
        return pl.ds(pl.multiple_of(j * tok, tok), tok)

    def copy_to(src, dst, ssem, rsem, dev):
        return pltpu.make_async_remote_copy(
            src_ref=src, dst_ref=dst, send_sem=ssem, recv_sem=rsem,
            device_id={"adapter": dev}, device_id_type=pl.DeviceIdType.MESH,
        )

    barrier = pltpu.get_barrier_semaphore()

    def greet(dev):
        pl.semaphore_signal(
            barrier, inc=1, device_id={"adapter": dev}, device_id_type=pl.DeviceIdType.MESH
        )

    for d in range(1, ny):
        greet(z * ny + peer(d))
    pl.when(z > 0)(lambda: greet(me - ny))
    pl.when(z < nz - 1)(lambda: greet(me + ny))
    pl.semaphore_wait(
        barrier,
        (ny - 1) + jnp.where(z > 0, 1, 0) + jnp.where(z < nz - 1, 1, 0),
    )

    sends = []

    def y_start(kind, d, src, dst):
        c = copy_to(
            src, dst, y_send.at[kind, d - 1], y_recv.at[kind, d - 1], z * ny + peer(d)
        )
        c.start()
        sends.append(c)

    def group(j):
        return pl.ds(pl.multiple_of(j * width, width), width)

    def y_start_columns(kind, d, src, dst):
        y_start(kind, d, src.at[:, group(peer(d))], dst)

    def y_wait(kind, d, dst):
        copy_to(
            dst, dst, y_send.at[kind, d - 1], y_recv.at[kind, d - 1], z * ny + back(d)
        ).wait_recv()

    for d in range(1, ny):
        y_start(0, d, b_ref, b_all.at[me])
    for d in range(1, ny):
        y_start_columns(1, d, x_ref, x_all.at[slot(y)])
    keep_b = pltpu.make_async_copy(b_ref, b_all.at[me], loc_sem.at[0])
    keep_og = pltpu.make_async_copy(og_ref, og_all.at[slot(y)], loc_sem.at[3])
    keep_b.start()
    keep_a = pltpu.make_async_copy(a_ref.at[:, group(y)], a_all.at[me], loc_sem.at[1])
    keep_x = pltpu.make_async_copy(x_ref.at[:, group(y)], x_all.at[slot(y)], loc_sem.at[2])
    keep_a.start()
    keep_x.start()
    keep_og.start()

    def hop(buf, ssem, rsem, s, ys, last=False):
        n_left = (z - s) * ny + ys
        n_right = (z + s) * ny + ys

        def right(start):
            c = copy_to(buf.at[n_left], buf.at[n_left], ssem.at[0, n_left], rsem.at[n_left], me + ny)
            c.start() if start else c.wait_send()

        def left(start):
            c = copy_to(
                buf.at[n_right], buf.at[n_right], ssem.at[1, n_right], rsem.at[n_right], me - ny
            )
            c.start() if start else c.wait_send()

        if last:
            pl.when((z >= s) & (z < nz - 1))(lambda: right(False))
            pl.when((z + s < nz) & (z > 0))(lambda: left(False))
            return
        if s > 0:
            @pl.when(z >= s)
            def _():
                copy_to(
                    buf.at[n_left], buf.at[n_left], ssem.at[0, n_left], rsem.at[n_left], me - ny
                ).wait_recv()
        pl.when((z >= s) & (z < nz - 1))(lambda: right(True))
        if s > 0:
            @pl.when(z + s < nz)
            def _():
                copy_to(
                    buf.at[n_right], buf.at[n_right], ssem.at[1, n_right], rsem.at[n_right], me + ny
                ).wait_recv()
        pl.when((z + s < nz) & (z > 0))(lambda: left(True))

    def hop_b(s):
        hop(b_all, b_send, b_recv, s, y)
        for d in range(1, ny):
            if s == 0:
                y_wait(0, d, b_all.at[z * ny + back(d)])
            hop(b_all, b_send, b_recv, s, back(d))

    def hop_own(s):
        hop(a_all, ag_send, ag_recv, s, y)

    def hop_peers(s):
        for d in range(1, ny):
            if s == 0:
                y_wait(2, d, a_all.at[z * ny + back(d)])
            hop(a_all, ag_send, ag_recv, s, back(d))

    keep_b.wait()
    hop_b(0)
    keep_a.wait()
    hop_own(0)
    hop_b(1)
    for s in range(2, nz):
        hop_b(s)
        if s < nz - 1:
            hop_own(s - 1)

    def masked(dense, n):
        adapter = n * owned + lax.broadcasted_iota(jnp.int32, dense.shape, 0) // rank
        return jnp.where(adapter == idx_ref[...], dense, 0.0).astype(jnp.bfloat16)

    def lg_block(n, carry):
        dense = adapter_scale * lax.dot_general(
            b_all[n], og_ref[...], NT, preferred_element_type=jnp.float32
        )
        lg_t[n, :, slot(y)] = masked(dense, n)
        return carry

    lax.fori_loop(0, nb, lg_block, 0)
    for d in range(1, ny):
        y_start(4, d, lg_t.at[:, :, slot(y)], lg_t.at[:, :, slot(y)])
    for d in range(1, ny):
        y_start_columns(2, d, a_ref, a_all.at[me])
    keep_og.wait()
    for d in range(1, ny):
        y_start(3, d, og_ref, og_all.at[slot(y)])
    keep_x.wait()
    for d in range(1, ny):
        y_wait(1, d, x_all.at[slot(back(d))])
        y_wait(4, d, lg_t.at[:, :, slot(back(d))])

    def grad(coef, acts, n, count, total, step, put, extra=()):
        blocks = pl.ds(n, count)

        @pl.loop(0, total // step)
        def _(i):
            start = pl.multiple_of(i * step, step)
            cols = pl.ds(start, step)
            acc = jnp.dot(
                coef[blocks].reshape(count * rows, coef.shape[2]), acts(cols),
                preferred_element_type=jnp.float32,
            )
            for ref, at in extra:
                acc += ref[pl.ds(at, count), :, cols].reshape(count * rows, step).astype(
                    jnp.float32
                )
            put(start, cols, acc)

    def x_acts(cols):
        return x_all[:, cols]

    def v_acts(cols):
        return og_all[:, pl.ds(pl.multiple_of(y * vcols, vcols), vcols)]

    def reduce_step(t, coef, acts, out, inbox, inbox2, ssem, rsem, rsem2, total, step, last=False):
        for right in (True, False):
            pos = z if right else nz - 1 - z
            zo = (nz - 1 - (t - z)) if right else (t - (nz - 1 - z))
            ahead = me + ny if right else me - ny
            behind = me - ny if right else me + ny

            @pl.when((pos <= t) & (pos < nz - 1))
            def _():
                blocks = pl.ds(zo * ny, ny)

                def send(dst, recv):
                    return copy_to(out.at[blocks], dst, ssem.at[zo], recv, ahead)

                if last:
                    send(inbox.at[blocks], rsem.at[zo]).wait_send()
                    return

                def put(start, cols, acc):
                    out[blocks, :, cols] = acc.astype(jnp.bfloat16).reshape(ny, rows, step)

                @pl.when(pos == 0)
                def _():
                    grad(coef, acts, zo * ny, ny, total, step, put)

                @pl.when(pos > 0)
                def _():
                    copy_to(
                        inbox.at[blocks], inbox.at[blocks], ssem.at[zo], rsem.at[zo], behind
                    ).wait_recv()
                    grad(coef, acts, zo * ny, ny, total, step, put, ((inbox, zo * ny),))

                if right:
                    send(inbox.at[blocks], rsem.at[zo]).start()
                else:
                    pl.when(zo == z - 1)(lambda: send(inbox2, rsem2.at[0]).start())
                    pl.when(zo < z - 1)(lambda: send(inbox.at[blocks], rsem.at[zo]).start())

    def reduce_end(coef, acts, own, out, inbox, inbox2, rsem, rsem2, total, step):
        blocks = pl.ds(z * ny, ny)

        @pl.when(z > 0)
        def _():
            copy_to(inbox.at[blocks], inbox.at[blocks], rsem.at[z], rsem.at[z], me - ny).wait_recv()

        @pl.when(z < nz - 1)
        def _():
            copy_to(inbox2, inbox2, rsem2.at[0], rsem2.at[0], me + ny).wait_recv()

        for d in range(1, ny + 1):
            yo = lax.rem(y + d, ny)
            n = z * ny + yo

            def put(start, cols, acc):
                if d == ny:
                    own(y, start, acc)
                else:
                    out[d - 1, :, cols] = acc.astype(jnp.bfloat16)

            first, second = (inbox, n), (inbox2, yo)

            @pl.when((z > 0) & (z < nz - 1))
            def _():
                grad(coef, acts, n, 1, total, step, put, (first, second))

            @pl.when(z == 0)
            def _():
                grad(coef, acts, n, 1, total, step, put, (second,))

            @pl.when(z == nz - 1)
            def _():
                grad(coef, acts, n, 1, total, step, put, (first,))

            yield d

    def down_at(j, start, values):
        dg_full[:, pl.ds(pl.multiple_of(j * width + start, tile), tile)] = values

    def up_at(j, start, values):
        up_full[:, pl.ds(pl.multiple_of(j * vcols, vcols), vcols)] = adapter_scale * values

    down = (lg_t, x_acts, gbuf, rin, rin2, rs_send, rs_recv, rs_recv2, width, tile)
    up = (low_all, v_acts, ubuf, uin, uin2, us_send, us_recv, us_recv2, vcols, vcols)
    reduce_step(0, *down)
    if nz > 2:
        hop_own(nz - 2)
    hop_peers(0)
    for s in range(1, nz - 1):
        hop_peers(s)
        reduce_step(s, *down)
    hop_own(nz - 1)
    hop_peers(nz - 1)

    for j in range(ny):
        low_part[j] = jnp.zeros((nb * rows, tok), jnp.float32)

        @pl.loop(0, width // tile)
        def _(i):
            cols = pl.ds(pl.multiple_of(i * tile, tile), tile)
            low_part[j] += lax.dot_general(
                a_all[:, :, cols].reshape(nb * rows, tile), x_all[slot(j), cols], NT,
                preferred_element_type=jnp.float32,
            )

    def side_rows(j, put):
        @pl.loop(0, width // tile)
        def _(i):
            start = pl.multiple_of(i * tile, tile)
            cols = pl.ds(start, tile)
            acc = lax.dot_general(
                lg_t[:, :, slot(j)].reshape(nb * rows, tok), a_all[:, :, cols].reshape(nb * rows, tile),
                (((0,), (0,)), ((), ())), preferred_element_type=jnp.float32,
            )
            put(start, cols, acc.astype(jnp.bfloat16))

    for d in range(1, ny):
        y_start(5, d, low_part.at[peer(d)], low_in.at[d - 1])
    for d in range(1, ny):
        def put_peer(start, cols, values):
            side_out[d - 1, :, cols] = values

        side_rows(peer(d), put_peer)
    for d in range(1, ny):
        y_wait(5, d, low_in.at[d - 1])

    def low_sum(n, carry):
        at = pl.ds(pl.multiple_of(n * rows, rows), rows)
        total = low_part[y, at]
        for d in range(1, ny):
            total += low_in[d - 1, at]
        low_all[n, :, slot(y)] = masked(total, n)
        return carry

    lax.fori_loop(0, nb, low_sum, 0)
    for d in range(1, ny):
        y_start(6, d, low_all.at[:, :, slot(y)], low_all.at[:, :, slot(y)])
    for d in range(1, ny):
        y_start(9, d, side_out.at[d - 1], side_full.at[:, group(y)])
    for d in range(1, ny):
        y_wait(3, d, og_all.at[slot(back(d))])
        y_wait(6, d, low_all.at[:, :, slot(back(d))])

    for t in range(nz - 1):
        reduce_step(t, *up)

    def put_own(start, cols, values):
        side_full[:, pl.ds(pl.multiple_of(y * width + start, tile), tile)] = values

    side_rows(y, put_own)
    for d in reduce_end(
        lg_t, x_acts, down_at, dg_out, rin, rin2, rs_recv, rs_recv2, width, tile
    ):
        if d < ny:
            y_start(7, d, dg_out.at[d - 1], dg_in.at[d - 1])
    for d in reduce_end(
        low_all, v_acts, up_at, up_out, uin, uin2, us_recv, us_recv2, vcols, vcols
    ):
        if d < ny:
            y_start(8, d, up_out.at[d - 1], up_in.at[d - 1])
    for d in range(1, ny):
        y_wait(8, d, up_in.at[d - 1])
        up_at(back(d), 0, up_in[d - 1].astype(jnp.float32))
    for d in range(1, ny):
        y_wait(7, d, dg_in.at[d - 1])

        @pl.loop(0, width // tile)
        def _(i):
            start = pl.multiple_of(i * tile, tile)
            down_at(back(d), start, dg_in[d - 1, :, pl.ds(start, tile)].astype(jnp.float32))

    for d in range(1, ny):
        y_wait(9, d, side_full.at[:, group(back(d))])
    for c in sends:
        c.wait_send()
    for s in range(nz):
        for d in range(ny):
            hop(b_all, b_send, b_recv, s, peer(d), last=True)
            hop(a_all, ag_send, ag_recv, s, peer(d), last=True)
    for t in range(nz - 1):
        reduce_step(t, *down, last=True)
        reduce_step(t, *up, last=True)


def exchange(nz, ny, rank, idx, a_rows, b_rows, tokens, grads):
    nb = nz * ny
    rows = a_rows.shape[0]
    width = a_rows.shape[1] // ny
    tok_rows = tokens.shape[0]
    kv_width = grads.shape[1]
    vcols = kv_width // ny
    bf, f32 = jnp.bfloat16, jnp.float32
    peers = max(1, ny - 1)
    outs = [
        ((nb, rows, kv_width), bf),
        ((nb, rows, ny * tok_rows), bf),
        ((tok_rows, ny * width), bf),
        ((rows, ny * width), f32),
        ((rows, kv_width), f32),
    ]
    vmem = pl.BlockSpec(memory_space=pltpu.VMEM)
    dma = pltpu.SemaphoreType.DMA
    return pl.pallas_call(
        functools.partial(exchange_kernel, nz, ny, rank, min(512, width)),
        out_shape=[jax.ShapeDtypeStruct(s, t) for s, t in outs],
        in_specs=[vmem] * 5,
        out_specs=[vmem] * len(outs),
        scratch_shapes=[
            pltpu.VMEM((nb, rows, width), bf),
            pltpu.VMEM((ny * tok_rows, width), bf),
            pltpu.VMEM((ny * tok_rows, kv_width), bf),
            pltpu.VMEM((nb, rows, ny * tok_rows), bf),
            pltpu.VMEM((peers, tok_rows, width), bf),
            pltpu.VMEM((nb, rows, width), bf),
            pltpu.VMEM((nb, rows, width), bf),
            pltpu.VMEM((ny, rows, width), bf),
            pltpu.VMEM((nb, rows, vcols), bf),
            pltpu.VMEM((nb, rows, vcols), bf),
            pltpu.VMEM((ny, rows, vcols), bf),
            pltpu.VMEM((ny, nb * rows, tok_rows), f32),
            pltpu.VMEM((peers, nb * rows, tok_rows), f32),
            pltpu.VMEM((peers, rows, width), bf),
            pltpu.VMEM((peers, rows, width), bf),
            pltpu.VMEM((peers, rows, vcols), bf),
            pltpu.VMEM((peers, rows, vcols), bf),
            dma((4,)),
            dma((2, nb)),
            dma((nb,)),
            dma((2, nb)),
            dma((nb,)),
            dma((10, peers)),
            dma((10, peers)),
            dma((nz,)),
            dma((nz,)),
            dma((1,)),
            dma((nz,)),
            dma((nz,)),
            dma((1,)),
        ],
        compiler_params=pltpu.CompilerParams(
            collective_id=0, has_side_effects=True, vmem_limit_bytes=60 * 1024 * 1024
        ),
    )(idx, a_rows, b_rows, tokens, grads)


def local(
    tokens,
    token_adapter_index,
    frozen_value_weight,
    adapter_down_factors,
    adapter_up_factors,
    output_gradient,
):
    owners = lax.axis_size("adapter")
    nz, ny = grid_sides(owners)
    owned, rank, width = adapter_down_factors.shape
    tok_rows = tokens.shape[0]
    kv_width = output_gradient.shape[1]
    y = lax.rem(lax.axis_index("adapter"), ny)
    weight = lax.all_gather(frozen_value_weight, "dp", axis=0, tiled=True)
    b_all, low_all, side, down_grad, up_factor_gradient = exchange(
        nz, ny, rank,
        token_adapter_index.reshape(1, tok_rows),
        adapter_down_factors.reshape(owned * rank, width),
        adapter_up_factors.reshape(owned * rank, kv_width),
        tokens,
        output_gradient,
    )
    slots = owners * owned * rank
    low_own = lax.dynamic_slice_in_dim(
        low_all.reshape(slots, ny * tok_rows), y * tok_rows, tok_rows, 1
    )
    lifted = (
        adapter_scale
        * lax.dot_general(
            low_own, b_all.reshape(slots, kv_width), (((0,), (0,)), ((), ())),
            preferred_element_type=jnp.float32,
        )
    ).astype(jnp.bfloat16)
    base = jnp.dot(tokens, weight, preferred_element_type=jnp.float32)
    back = lax.dot_general(
        output_gradient, weight, (((1,), (1,)), ((), ())), preferred_element_type=jnp.float32
    )
    return (
        (base + lifted).astype(jnp.bfloat16),
        (back + side).astype(jnp.bfloat16),
        down_grad.reshape(owned, rank, width),
        up_factor_gradient.reshape(owned, rank, kv_width),
    )


def solution(mesh):
    in_specs = (
        P(("dp", "adapter"), None),
        P(("dp", "adapter"), None),
        P("dp", None),
        P(("dp", "adapter"), None, None),
        P(("dp", "adapter"), None, None),
        P(("dp", "adapter"), None),
    )
    out_specs = (
        P(("dp", "adapter"), None),
        P(("dp", "adapter"), None),
        P(("dp", "adapter"), None, None),
        P(("dp", "adapter"), None, None),
    )
    return jax.shard_map(local, mesh=mesh, in_specs=in_specs, out_specs=out_specs, check_vma=False)
```

```python
import functools

import jax
import jax.numpy as jnp
from jax import lax
from jax.experimental import pallas as pl
from jax.experimental.pallas import tpu as pltpu
from jax.sharding import PartitionSpec as P

adapter_scale = 2.0
NT = (((1,), (1,)), ((), ()))


def grid_sides(owners):
    ny = 1
    while (2 * ny) ** 2 <= owners:
        ny *= 2
    return owners // ny, ny


def exchange_kernel(
    nz, ny, rank, tile,
    idx_ref, a_ref, b_ref, x_ref, og_ref,
    b_all, low_all, side_full, dg_full, up_full,
    a_all, x_all, og_all, lg_t, side_out, gbuf, rin, rin2, ubuf, uin, uin2, low_part, low_in, dg_out, dg_in, up_out, up_in,
    loc_sem, ag_send, ag_recv, b_send, b_recv, y_send, y_recv,
    rs_send, rs_recv, rs_recv2, us_send, us_recv, us_recv2,
):
    me = lax.axis_index("adapter")
    z = me // ny
    y = lax.rem(me, ny)
    rows, width = a_all.shape[1:]
    tok = og_ref.shape[0]
    vcols = ubuf.shape[2]
    owned = rows // rank
    nb = nz * ny

    def peer(d):
        return lax.rem(y + d, ny)

    def back(d):
        return lax.rem(y + ny - d, ny)

    def slot(j):
        return pl.ds(pl.multiple_of(j * tok, tok), tok)

    def copy_to(src, dst, ssem, rsem, dev):
        return pltpu.make_async_remote_copy(
            src_ref=src, dst_ref=dst, send_sem=ssem, recv_sem=rsem,
            device_id={"adapter": dev}, device_id_type=pl.DeviceIdType.MESH,
        )

    barrier = pltpu.get_barrier_semaphore()

    def greet(dev):
        pl.semaphore_signal(
            barrier, inc=1, device_id={"adapter": dev}, device_id_type=pl.DeviceIdType.MESH
        )

    for d in range(1, ny):
        greet(z * ny + peer(d))
    pl.when(z > 0)(lambda: greet(me - ny))
    pl.when(z < nz - 1)(lambda: greet(me + ny))
    pl.semaphore_wait(
        barrier,
        (ny - 1) + jnp.where(z > 0, 1, 0) + jnp.where(z < nz - 1, 1, 0),
    )

    sends = []

    def y_start(kind, d, src, dst):
        c = copy_to(
            src, dst, y_send.at[kind, d - 1], y_recv.at[kind, d - 1], z * ny + peer(d)
        )
        c.start()
        sends.append(c)

    def group(j):
        return pl.ds(pl.multiple_of(j * width, width), width)

    def y_start_columns(kind, d, src, dst):
        y_start(kind, d, src.at[:, group(peer(d))], dst)

    def y_wait(kind, d, dst):
        copy_to(
            dst, dst, y_send.at[kind, d - 1], y_recv.at[kind, d - 1], z * ny + back(d)
        ).wait_recv()

    for d in range(1, ny):
        y_start(0, d, b_ref, b_all.at[me])
    for d in range(1, ny):
        y_start_columns(1, d, x_ref, x_all.at[slot(y)])
    keep_b = pltpu.make_async_copy(b_ref, b_all.at[me], loc_sem.at[0])
    keep_og = pltpu.make_async_copy(og_ref, og_all.at[slot(y)], loc_sem.at[3])
    keep_b.start()
    keep_a = pltpu.make_async_copy(a_ref.at[:, group(y)], a_all.at[me], loc_sem.at[1])
    keep_x = pltpu.make_async_copy(x_ref.at[:, group(y)], x_all.at[slot(y)], loc_sem.at[2])
    keep_a.start()
    keep_x.start()
    keep_og.start()

    def hop(buf, ssem, rsem, s, ys, last=False):
        n_left = (z - s) * ny + ys
        n_right = (z + s) * ny + ys

        def right(start):
            c = copy_to(buf.at[n_left], buf.at[n_left], ssem.at[0, n_left], rsem.at[n_left], me + ny)
            c.start() if start else c.wait_send()

        def left(start):
            c = copy_to(
                buf.at[n_right], buf.at[n_right], ssem.at[1, n_right], rsem.at[n_right], me - ny
            )
            c.start() if start else c.wait_send()

        if last:
            pl.when((z >= s) & (z < nz - 1))(lambda: right(False))
            pl.when((z + s < nz) & (z > 0))(lambda: left(False))
            return
        if s > 0:
            @pl.when(z >= s)
            def _():
                copy_to(
                    buf.at[n_left], buf.at[n_left], ssem.at[0, n_left], rsem.at[n_left], me - ny
                ).wait_recv()
        pl.when((z >= s) & (z < nz - 1))(lambda: right(True))
        if s > 0:
            @pl.when(z + s < nz)
            def _():
                copy_to(
                    buf.at[n_right], buf.at[n_right], ssem.at[1, n_right], rsem.at[n_right], me + ny
                ).wait_recv()
        pl.when((z + s < nz) & (z > 0))(lambda: left(True))

    def hop_b(s):
        hop(b_all, b_send, b_recv, s, y)
        for d in range(1, ny):
            if s == 0:
                y_wait(0, d, b_all.at[z * ny + back(d)])
            hop(b_all, b_send, b_recv, s, back(d))

    def hop_own(s):
        hop(a_all, ag_send, ag_recv, s, y)

    def hop_peers(s):
        for d in range(1, ny):
            if s == 0:
                y_wait(2, d, a_all.at[z * ny + back(d)])
            hop(a_all, ag_send, ag_recv, s, back(d))

    keep_b.wait()
    hop_b(0)
    keep_a.wait()
    hop_own(0)
    for d in range(1, ny):
        y_start_columns(2, d, a_ref, a_all.at[me])
    hop_b(1)
    for s in range(2, nz):
        hop_b(s)
        if s < nz - 1:
            hop_own(s - 1)

    def masked(dense, n):
        adapter = n * owned + lax.broadcasted_iota(jnp.int32, dense.shape, 0) // rank
        return jnp.where(adapter == idx_ref[...], dense, 0.0).astype(jnp.bfloat16)

    def lg_block(n, carry):
        dense = adapter_scale * lax.dot_general(
            b_all[n], og_ref[...], NT, preferred_element_type=jnp.float32
        )
        lg_t[n, :, slot(y)] = masked(dense, n)
        return carry

    lax.fori_loop(0, nb, lg_block, 0)
    for d in range(1, ny):
        y_start(4, d, lg_t.at[:, :, slot(y)], lg_t.at[:, :, slot(y)])
    keep_og.wait()
    for d in range(1, ny):
        y_start(3, d, og_ref, og_all.at[slot(y)])
    keep_x.wait()
    for d in range(1, ny):
        y_wait(1, d, x_all.at[slot(back(d))])
        y_wait(4, d, lg_t.at[:, :, slot(back(d))])

    def grad(coef, acts, n, count, total, step, put, extra=()):
        blocks = pl.ds(n, count)

        @pl.loop(0, total // step)
        def _(i):
            start = pl.multiple_of(i * step, step)
            cols = pl.ds(start, step)
            acc = jnp.dot(
                coef[blocks].reshape(count * rows, coef.shape[2]), acts(cols),
                preferred_element_type=jnp.float32,
            )
            for ref, at in extra:
                acc += ref[pl.ds(at, count), :, cols].reshape(count * rows, step).astype(
                    jnp.float32
                )
            put(start, cols, acc)

    def x_acts(cols):
        return x_all[:, cols]

    def v_acts(cols):
        return og_all[:, pl.ds(pl.multiple_of(y * vcols, vcols), vcols)]

    def reduce_step(t, coef, acts, out, inbox, inbox2, ssem, rsem, rsem2, total, step, last=False):
        for right in (True, False):
            pos = z if right else nz - 1 - z
            zo = (nz - 1 - (t - z)) if right else (t - (nz - 1 - z))
            ahead = me + ny if right else me - ny
            behind = me - ny if right else me + ny

            @pl.when((pos <= t) & (pos < nz - 1))
            def _():
                blocks = pl.ds(zo * ny, ny)

                def send(dst, recv):
                    return copy_to(out.at[blocks], dst, ssem.at[zo], recv, ahead)

                if last:
                    send(inbox.at[blocks], rsem.at[zo]).wait_send()
                    return

                def put(start, cols, acc):
                    out[blocks, :, cols] = acc.astype(jnp.bfloat16).reshape(ny, rows, step)

                @pl.when(pos == 0)
                def _():
                    grad(coef, acts, zo * ny, ny, total, step, put)

                @pl.when(pos > 0)
                def _():
                    copy_to(
                        inbox.at[blocks], inbox.at[blocks], ssem.at[zo], rsem.at[zo], behind
                    ).wait_recv()
                    grad(coef, acts, zo * ny, ny, total, step, put, ((inbox, zo * ny),))

                if right:
                    send(inbox.at[blocks], rsem.at[zo]).start()
                else:
                    pl.when(zo == z - 1)(lambda: send(inbox2, rsem2.at[0]).start())
                    pl.when(zo < z - 1)(lambda: send(inbox.at[blocks], rsem.at[zo]).start())

    def reduce_end(coef, acts, own, out, inbox, inbox2, rsem, rsem2, total, step):
        blocks = pl.ds(z * ny, ny)

        @pl.when(z > 0)
        def _():
            copy_to(inbox.at[blocks], inbox.at[blocks], rsem.at[z], rsem.at[z], me - ny).wait_recv()

        @pl.when(z < nz - 1)
        def _():
            copy_to(inbox2, inbox2, rsem2.at[0], rsem2.at[0], me + ny).wait_recv()

        for d in range(1, ny + 1):
            yo = lax.rem(y + d, ny)
            n = z * ny + yo

            def put(start, cols, acc):
                if d == ny:
                    own(y, start, acc)
                else:
                    out[d - 1, :, cols] = acc.astype(jnp.bfloat16)

            first, second = (inbox, n), (inbox2, yo)

            @pl.when((z > 0) & (z < nz - 1))
            def _():
                grad(coef, acts, n, 1, total, step, put, (first, second))

            @pl.when(z == 0)
            def _():
                grad(coef, acts, n, 1, total, step, put, (second,))

            @pl.when(z == nz - 1)
            def _():
                grad(coef, acts, n, 1, total, step, put, (first,))

            yield d

    def down_at(j, start, values):
        dg_full[:, pl.ds(pl.multiple_of(j * width + start, tile), tile)] = values

    def up_at(j, start, values):
        up_full[:, pl.ds(pl.multiple_of(j * vcols, vcols), vcols)] = adapter_scale * values

    down = (lg_t, x_acts, gbuf, rin, rin2, rs_send, rs_recv, rs_recv2, width, tile)
    up = (low_all, v_acts, ubuf, uin, uin2, us_send, us_recv, us_recv2, vcols, vcols)
    reduce_step(0, *down)
    if nz > 2:
        hop_own(nz - 2)
    hop_peers(0)
    for s in range(1, nz - 1):
        hop_peers(s)
        reduce_step(s, *down)
    hop_own(nz - 1)
    hop_peers(nz - 1)

    for j in range(ny):
        low_part[j] = jnp.zeros((nb * rows, tok), jnp.float32)

        @pl.loop(0, width // tile)
        def _(i):
            cols = pl.ds(pl.multiple_of(i * tile, tile), tile)
            low_part[j] += lax.dot_general(
                a_all[:, :, cols].reshape(nb * rows, tile), x_all[slot(j), cols], NT,
                preferred_element_type=jnp.float32,
            )

    def side_rows(j, put):
        @pl.loop(0, width // tile)
        def _(i):
            start = pl.multiple_of(i * tile, tile)
            cols = pl.ds(start, tile)
            acc = lax.dot_general(
                lg_t[:, :, slot(j)].reshape(nb * rows, tok), a_all[:, :, cols].reshape(nb * rows, tile),
                (((0,), (0,)), ((), ())), preferred_element_type=jnp.float32,
            )
            put(start, cols, acc.astype(jnp.bfloat16))

    for d in range(1, ny):
        y_start(5, d, low_part.at[peer(d)], low_in.at[d - 1])
    for d in range(1, ny):
        def put_peer(start, cols, values):
            side_out[d - 1, :, cols] = values

        side_rows(peer(d), put_peer)
    for d in range(1, ny):
        y_wait(5, d, low_in.at[d - 1])

    def low_sum(n, carry):
        at = pl.ds(pl.multiple_of(n * rows, rows), rows)
        total = low_part[y, at]
        for d in range(1, ny):
            total += low_in[d - 1, at]
        low_all[n, :, slot(y)] = masked(total, n)
        return carry

    lax.fori_loop(0, nb, low_sum, 0)
    for d in range(1, ny):
        y_start(6, d, low_all.at[:, :, slot(y)], low_all.at[:, :, slot(y)])
    for d in range(1, ny):
        y_start(9, d, side_out.at[d - 1], side_full.at[:, group(y)])
    for d in range(1, ny):
        y_wait(3, d, og_all.at[slot(back(d))])
        y_wait(6, d, low_all.at[:, :, slot(back(d))])

    for t in range(nz - 1):
        reduce_step(t, *up)

    def put_own(start, cols, values):
        side_full[:, pl.ds(pl.multiple_of(y * width + start, tile), tile)] = values

    side_rows(y, put_own)
    for d in reduce_end(
        lg_t, x_acts, down_at, dg_out, rin, rin2, rs_recv, rs_recv2, width, tile
    ):
        if d < ny:
            y_start(7, d, dg_out.at[d - 1], dg_in.at[d - 1])
    for d in reduce_end(
        low_all, v_acts, up_at, up_out, uin, uin2, us_recv, us_recv2, vcols, vcols
    ):
        if d < ny:
            y_start(8, d, up_out.at[d - 1], up_in.at[d - 1])
    for d in range(1, ny):
        y_wait(8, d, up_in.at[d - 1])
        up_at(back(d), 0, up_in[d - 1].astype(jnp.float32))
    for d in range(1, ny):
        y_wait(7, d, dg_in.at[d - 1])

        @pl.loop(0, width // tile)
        def _(i):
            start = pl.multiple_of(i * tile, tile)
            down_at(back(d), start, dg_in[d - 1, :, pl.ds(start, tile)].astype(jnp.float32))

    for d in range(1, ny):
        y_wait(9, d, side_full.at[:, group(back(d))])
    for c in sends:
        c.wait_send()
    for s in range(nz):
        for d in range(ny):
            hop(b_all, b_send, b_recv, s, peer(d), last=True)
            hop(a_all, ag_send, ag_recv, s, peer(d), last=True)
    for t in range(nz - 1):
        reduce_step(t, *down, last=True)
        reduce_step(t, *up, last=True)


def exchange(nz, ny, rank, idx, a_rows, b_rows, tokens, grads):
    nb = nz * ny
    rows = a_rows.shape[0]
    width = a_rows.shape[1] // ny
    tok_rows = tokens.shape[0]
    kv_width = grads.shape[1]
    vcols = kv_width // ny
    bf, f32 = jnp.bfloat16, jnp.float32
    peers = max(1, ny - 1)
    outs = [
        ((nb, rows, kv_width), bf),
        ((nb, rows, ny * tok_rows), bf),
        ((tok_rows, ny * width), bf),
        ((rows, ny * width), f32),
        ((rows, kv_width), f32),
    ]
    vmem = pl.BlockSpec(memory_space=pltpu.VMEM)
    dma = pltpu.SemaphoreType.DMA
    return pl.pallas_call(
        functools.partial(exchange_kernel, nz, ny, rank, min(512, width)),
        out_shape=[jax.ShapeDtypeStruct(s, t) for s, t in outs],
        in_specs=[vmem] * 5,
        out_specs=[vmem] * len(outs),
        scratch_shapes=[
            pltpu.VMEM((nb, rows, width), bf),
            pltpu.VMEM((ny * tok_rows, width), bf),
            pltpu.VMEM((ny * tok_rows, kv_width), bf),
            pltpu.VMEM((nb, rows, ny * tok_rows), bf),
            pltpu.VMEM((peers, tok_rows, width), bf),
            pltpu.VMEM((nb, rows, width), bf),
            pltpu.VMEM((nb, rows, width), bf),
            pltpu.VMEM((ny, rows, width), bf),
            pltpu.VMEM((nb, rows, vcols), bf),
            pltpu.VMEM((nb, rows, vcols), bf),
            pltpu.VMEM((ny, rows, vcols), bf),
            pltpu.VMEM((ny, nb * rows, tok_rows), f32),
            pltpu.VMEM((peers, nb * rows, tok_rows), f32),
            pltpu.VMEM((peers, rows, width), bf),
            pltpu.VMEM((peers, rows, width), bf),
            pltpu.VMEM((peers, rows, vcols), bf),
            pltpu.VMEM((peers, rows, vcols), bf),
            dma((4,)),
            dma((2, nb)),
            dma((nb,)),
            dma((2, nb)),
            dma((nb,)),
            dma((10, peers)),
            dma((10, peers)),
            dma((nz,)),
            dma((nz,)),
            dma((1,)),
            dma((nz,)),
            dma((nz,)),
            dma((1,)),
        ],
        compiler_params=pltpu.CompilerParams(
            collective_id=0, has_side_effects=True, vmem_limit_bytes=60 * 1024 * 1024
        ),
    )(idx, a_rows, b_rows, tokens, grads)


def local(
    tokens,
    token_adapter_index,
    frozen_value_weight,
    adapter_down_factors,
    adapter_up_factors,
    output_gradient,
):
    owners = lax.axis_size("adapter")
    nz, ny = grid_sides(owners)
    owned, rank, width = adapter_down_factors.shape
    tok_rows = tokens.shape[0]
    kv_width = output_gradient.shape[1]
    y = lax.rem(lax.axis_index("adapter"), ny)
    weight = lax.all_gather(frozen_value_weight, "dp", axis=0, tiled=True)
    b_all, low_all, side, down_grad, up_factor_gradient = exchange(
        nz, ny, rank,
        token_adapter_index.reshape(1, tok_rows),
        adapter_down_factors.reshape(owned * rank, width),
        adapter_up_factors.reshape(owned * rank, kv_width),
        tokens,
        output_gradient,
    )
    slots = owners * owned * rank
    low_own = lax.dynamic_slice_in_dim(
        low_all.reshape(slots, ny * tok_rows), y * tok_rows, tok_rows, 1
    )
    lifted = (
        adapter_scale
        * lax.dot_general(
            low_own, b_all.reshape(slots, kv_width), (((0,), (0,)), ((), ())),
            preferred_element_type=jnp.float32,
        )
    ).astype(jnp.bfloat16)
    base = jnp.dot(tokens, weight, preferred_element_type=jnp.float32)
    back = lax.dot_general(
        output_gradient, weight, (((1,), (1,)), ((), ())), preferred_element_type=jnp.float32
    )
    return (
        (base + lifted).astype(jnp.bfloat16),
        (back + side).astype(jnp.bfloat16),
        down_grad.reshape(owned, rank, width),
        up_factor_gradient.reshape(owned, rank, kv_width),
    )


def solution(mesh):
    in_specs = (
        P(("dp", "adapter"), None),
        P(("dp", "adapter"), None),
        P("dp", None),
        P(("dp", "adapter"), None, None),
        P(("dp", "adapter"), None, None),
        P(("dp", "adapter"), None),
    )
    out_specs = (
        P(("dp", "adapter"), None),
        P(("dp", "adapter"), None),
        P(("dp", "adapter"), None, None),
        P(("dp", "adapter"), None, None),
    )
    return jax.shard_map(local, mesh=mesh, in_specs=in_specs, out_specs=out_specs, check_vma=False)
```
